32 devices in a mesh: groups: 2 (over x), dp: 2 (over core), tensor: 8 (over z, y).
Axes of the slice: x: 2, y: 2, z: 4, core: 2. Of those that a mesh axis runs over, the one named last changes fastest.
Arguments:
- hidden: bfloat16 [4096, 5120], P(('groups', 'dp')), parts along dimension 0, may hold values from -6 to 6
- context: bfloat16 [4096, 5120], P(('groups', 'dp'), 'tensor'), parts along dimension 0, may hold values from -6 to 6
- w_qkv: bfloat16 [5120, 7168], P(None, 'tensor'), may hold values from -0.078125 to 0.078125
- w_out: bfloat16 [5120, 5120], P('tensor'), may hold values from -0.078125 to 0.078125
- a_qkv: bfloat16 [16, 5120, 64], P(('dp', 'tensor')), may hold values from -0.078125 to 0.078125
- b_qkv: bfloat16 [16, 64, 7168], P(('dp', 'tensor')), may hold values from -0.75 to 0.75
- a_out: bfloat16 [16, 5120, 64], P(('dp', 'tensor')), may hold values from -0.078125 to 0.078125
- b_out: bfloat16 [16, 64, 5120], P(('dp', 'tensor')), may hold values from -0.75 to 0.75
- seg_len: int32 [4, 32], P(('groups', 'dp')), parts along dimension 0, may hold values from 1 to 256, 1024 in all within a row
- seg_use: int32 [4, 32], P(('groups', 'dp')), parts along dimension 0, may hold values from 0 to 5
- used_list: int32 [4, 6], P('groups'), parts along dimension 0, may hold values from 0 to 15, as said below
- adapter_slot: int32 [16], replicated, may hold values from 0 to 15, each once
Outputs:
- qkv: bfloat16 [4096, 7168], P(('groups', 'dp'), 'tensor'), parts along dimension 0
- attn_out: bfloat16 [4096, 5120], P(('groups', 'dp'), 'tensor'), parts along dimension 0
The draws below stay inside these ranges and needn't reach their ends.
There are 2 independent parts, one for each index of `groups`. The reference program is written for one: setup_inputs(seed, part) draws one part's arguments, and reference() takes and returns one part's arrays. A program takes and returns all parts, laid end to end along the dimension named above; an argument that names none is the same for every part. Nothing has to cross between parts.
Inputs may be any that keep to these rules, and one draw needn't show every extreme that they name: `used_list`: each row holds 6 different adapter ids.
All inputs are finite; a program needn't handle non-finite values.
Results may differ from the reference program's by a relative error of at most 0.007.
Values may be sent and summed in bfloat16 or wider, within the bound.
A program may use at most 192 MiB of HBM per device.

```python
import math
import jax
import jax.numpy as jnp
import numpy as np
from jax import lax

D = 5120
QKV = 7168
RANK = 64
TOK_DEV = 1024
SEGS = 32
ADAPTERS = 16
USED = 6
DP_SHARDS = 2
TOKENS = 2048
MOST_SEG = 256


def draw_used_list(key, part):
    key = jax.random.fold_in(key, 11)
    row_keys = jax.random.split(key, DP_SHARDS)

    def one_row(row_key):
        return jax.random.permutation(row_key, ADAPTERS)[:USED]
    return jax.vmap(one_row)(row_keys).astype(jnp.int32)


def plant(values, key, smallest, top_value):
    extent = values.shape
    index_at = [jax.random.randint(jax.random.fold_in(key, axis), (), 0, extent[axis]) for axis in range(len(extent))]
    values = values.at[tuple(index_at)].set(smallest)
    longest = extent.index(max(extent))
    index_at[longest] = (index_at[longest] + 1) % extent[longest]
    return values.at[tuple(index_at)].set(top_value)


def steps_of(own_key, extent, pieces, low, top_value):
    def one(position, parts):
        heights = jax.random.uniform(jax.random.fold_in(jax.random.fold_in(own_key, 6), position), (parts,), jnp.float32, low / len(pieces), top_value / len(pieces))
        return jnp.repeat(jnp.exp(heights), extent[position] // parts).reshape((-1,) + (1,) * (len(extent) - position - 1))

    level = one(*pieces[0])
    for cut in pieces[1:]:
        level = level * one(*cut)
    return level


def profile(number_of, total, most, skew):
    loads = [(1 << 20) // math.isqrt(grade ** skew) + 1 for grade in range(2, number_of + 1)]
    spare, counts = total - most - (number_of - 1), [1] * (number_of - 1)
    while spare > 0:
        movable = [i for i in range(number_of - 1) if counts[i] < most]
        mass, left = sum([loads[i] for i in movable]), spare
        for i in movable:
            more = min(most - counts[i], max(1, left * loads[i] // mass), spare)
            counts[i] = counts[i] + more
            spare = spare - more
    return np.array([most] + counts)


def ragged_sizes(stream_key, count, total, most, slope):
    if count == 2:
        one = jax.random.randint(stream_key, (), max(1, total - most), min(most, total - 1) + 1)
        return jnp.stack([one, total - one])
    sizes = jnp.asarray(profile(count, total, most, slope), jnp.int32)
    couples = (count - 1) // 2
    donor, sink = sizes[1:1 + 2 * couples:2], sizes[2:2 + 2 * couples:2]
    margin = jnp.minimum(donor - 1, most - sink)
    moved = jax.random.randint(jax.random.fold_in(stream_key, 1), (couples,), 0, 1 << 20) % (margin + 1)
    sizes = sizes.at[1:1 + 2 * couples:2].set(donor - moved).at[2:2 + 2 * couples:2].set(sink + moved)
    return sizes[jax.random.permutation(jax.random.fold_in(stream_key, 2), count)]


def bell_draw(stream_key, dims, deviation, bound, shards=(), kind=jnp.bfloat16):
    values = deviation * jax.random.normal(stream_key, dims, jnp.float32)
    if shards:
        values = values * steps_of(stream_key, dims, shards, -0.22, 0.18)
    return jnp.clip(values, -bound, bound).astype(kind)


def setup_inputs(seed: int = 0, part: int = 0) -> dict:
    streams_of = jax.random.split(jax.random.key(seed), 13)
    part_splits = jax.random.split(jax.random.fold_in(streams_of[12], part), 13)
    return {
        "hidden": bell_draw(part_splits[0], (TOKENS, D), 1.0, 6.0, ((0, 2),)),
        "context": bell_draw(part_splits[1], (TOKENS, D), 1.0, 6.0, ((0, 2), (1, 8))),
        "w_qkv": bell_draw(streams_of[2], (D, QKV), D ** -0.5, 0.078125, ((1, 8),)),
        "w_out": bell_draw(streams_of[3], (D, D), D ** -0.5, 0.078125, ((0, 8),)),
        "a_qkv": bell_draw(streams_of[4], (ADAPTERS, D, RANK), D ** -0.5, 0.078125, ((0, 16),)),
        "b_qkv": bell_draw(streams_of[5], (ADAPTERS, RANK, QKV), RANK ** -0.5, 0.75, ((0, 16),)),
        "a_out": bell_draw(streams_of[6], (ADAPTERS, D, RANK), D ** -0.5, 0.078125, ((0, 16),)),
        "b_out": bell_draw(streams_of[7], (ADAPTERS, RANK, D), RANK ** -0.5, 0.75, ((0, 16),)),
        "seg_len": jax.vmap(lambda own: ragged_sizes(own, SEGS, TOK_DEV, MOST_SEG, 2))(jax.random.split(part_splits[8], DP_SHARDS)).reshape((DP_SHARDS, SEGS)).astype(jnp.int32),
        "seg_use": plant(jax.random.randint(part_splits[9], (DP_SHARDS, SEGS), 0, USED), jax.random.fold_in(part_splits[9], 1), 0, USED - 1).astype(jnp.int32),
        "used_list": draw_used_list(jax.random.fold_in(jax.random.fold_in(streams_of[12], part), 71), part),
        "adapter_slot": jax.random.permutation(streams_of[11], ADAPTERS).astype(jnp.int32),
    }


def token_rows(seg_len, seg_use, used_list, adapter_slot):
    seg_ends = jnp.cumsum(seg_len, axis=1)
    positions = jnp.arange(TOK_DEV, dtype=jnp.int32)
    segment = jnp.sum((positions[None, :, None] >= seg_ends[:, None, :]).astype(jnp.int32), axis=2)
    slot_tok = jnp.take_along_axis(seg_use, segment, axis=1)
    adapter = jnp.take_along_axis(used_list, slot_tok, axis=1)
    return adapter_slot[adapter].reshape(TOKENS)


def shrink(inputs, down_maps, token_mask):
    stacked = jnp.transpose(down_maps.astype(jnp.float32), (1, 0, 2)).reshape(D, ADAPTERS * RANK)
    products = jnp.dot(inputs.astype(jnp.float32), stacked, precision=lax.Precision.HIGHEST)
    products = products.reshape(TOKENS, ADAPTERS, RANK)
    return jnp.sum(products * token_mask[:, :, None], axis=1)


def expand(low_rank, up_maps, token_mask):
    spread = (token_mask[:, :, None] * low_rank.astype(jnp.float32)[:, None, :]).reshape(TOKENS, ADAPTERS * RANK)
    stacked = up_maps.astype(jnp.float32).reshape(ADAPTERS * RANK, up_maps.shape[2])
    return jnp.dot(spread, stacked, precision=lax.Precision.HIGHEST)


def reference(hidden, context, w_qkv, w_out, a_qkv, b_qkv, a_out, b_out, seg_len, seg_use, used_list, adapter_slot):
    store_row = token_rows(seg_len, seg_use, used_list, adapter_slot)
    token_mask = (store_row[:, None] == jnp.arange(ADAPTERS, dtype=jnp.int32)[None, :]).astype(jnp.float32)
    low_qkv = shrink(hidden, a_qkv, token_mask).astype(jnp.bfloat16)
    low_out = shrink(context, a_out, token_mask).astype(jnp.bfloat16)
    base_qkv = jnp.dot(hidden, w_qkv, preferred_element_type=jnp.float32)
    qkv = (base_qkv + expand(low_qkv, b_qkv, token_mask)).astype(jnp.bfloat16)
    base_out = jnp.dot(context, w_out, preferred_element_type=jnp.float32)
    attn_out = (base_out + expand(low_out, b_out, token_mask)).astype(jnp.bfloat16)
    return qkv, attn_out
```

```python
import jax
import jax.numpy as jnp
from jax import lax
from jax.sharding import PartitionSpec as P


def chunk_order(depth):
    rows = []
    for z in range(depth):
        row = []
        for s in range(depth - 1):
            for d, ok in ((z + depth - 1 - s, s >= z), (z - depth + 1 + s, s >= depth - 1 - z)):
                if ok:
                    row.append(d)
        rows.append(row + [z])
    return rows


def token_rows(seg_len, seg_use, row_of_use, tok_rows):
    count = seg_len.shape[0]
    order = jnp.arange(count, dtype=jnp.int32)
    ends = jnp.sum(jnp.where(order[None, :] <= order[:, None], seg_len[None, :], 0), axis=1)
    used = jnp.arange(row_of_use.shape[0], dtype=jnp.int32)
    seg_row = jnp.sum(jnp.where(seg_use[:, None] == used[None, :], row_of_use[None, :], 0), axis=1)
    positions = jnp.arange(tok_rows, dtype=jnp.int32)
    inside = (positions[:, None] >= (ends - seg_len)[None, :]) & (positions[:, None] < ends[None, :])
    return jnp.sum(jnp.where(inside, seg_row[None, :], 0), axis=1)


def shards(
    hidden,
    context,
    w_qkv,
    w_out,
    a_qkv,
    b_qkv,
    a_out,
    b_out,
    seg_len,
    seg_use,
    used_list,
    adapter_slot,
):
    f32, bf16 = jnp.float32, jnp.bfloat16
    tensor_size = lax.axis_size("tensor")
    dp_size = lax.axis_size("dp")
    t = lax.axis_index("tensor")
    dp_rank = lax.axis_index("dp")
    tok_rows, model_width = hidden.shape
    owned, _, rank = a_qkv.shape
    out_part = model_width // tensor_size
    qkv_part = b_qkv.shape[2] // tensor_size
    depth = tensor_size // 2
    z, y = t // 2, t % 2

    used = used_list[dp_rank][:, None] == jnp.arange(adapter_slot.shape[0], dtype=jnp.int32)[None, :]
    row_of_use = jnp.sum(jnp.where(used, adapter_slot[None, :], 0), axis=1)
    store_row = token_rows(seg_len[0], seg_use[0], row_of_use, tok_rows)

    def out_cols(d, side):
        return lax.dynamic_slice_in_dim(w_out, (2 * d + side) * out_part, out_part, 1)

    def partial(d, side):
        return jnp.dot(context, out_cols(d, side), preferred_element_type=f32)

    order = jnp.asarray(chunk_order(depth), jnp.int32)[z]
    swap = [(i, i ^ 1) for i in range(tensor_size)]
    both = [(0, 1), (1, 0)]

    def split(maps, part):
        return jnp.transpose(maps.reshape(owned, rank, tensor_size, part), (2, 0, 1, 3))

    a_out_t = jnp.transpose(a_out, (0, 2, 1))
    sent = jnp.concatenate(
        (split(a_out_t, out_part), split(b_out, out_part), split(b_qkv, qkv_part)), axis=3
    )

    reduced, up, down = [], None, None

    def chosen(d):
        value = reduced[0]
        for k in range(1, len(reduced)):
            value = jnp.where(order[k] == d, reduced[k], value)
        return value

    for k in range(depth):
        mine = lax.ppermute(partial(order[k], 1 - y).astype(bf16), "tensor", swap)
        reduced.append(mine.astype(f32) + partial(order[k], y))
        if k < depth - 1:
            s = k
            outgoing_up = chosen(z + depth - 1 - s)
            outgoing_down = chosen(z - depth + 1 + s)
            if s > 0:
                outgoing_up = outgoing_up + up.astype(f32)
                outgoing_down = outgoing_down + down.astype(f32)
            up_pairs = [(2 * i + j, 2 * i + 2 + j) for i in range(s + 1) for j in range(2)]
            down_pairs = [
                (2 * i + j, 2 * i - 2 + j) for i in range(depth - 1 - s, depth) for j in range(2)
            ]
            up = lax.ppermute(outgoing_up.astype(bf16), "tensor", up_pairs)
            down = lax.ppermute(outgoing_down.astype(bf16), "tensor", down_pairs)
        if k == 0:
            got = lax.all_to_all(sent, "tensor", split_axis=0, concat_axis=0, tiled=True)
            got = got.reshape((tensor_size * owned,) + got.shape[2:])
            other = lax.ppermute(got, "dp", both)
            a_other = lax.ppermute(a_qkv, "dp", both)
    base_out = reduced[-1] + up.astype(f32) + down.astype(f32)

    half = tensor_size * owned
    first = dp_rank * half
    second = (1 - dp_rank) * half
    rows = jnp.arange(half, dtype=jnp.int32)
    row_ids = jnp.concatenate((first + rows, second + rows))
    maps = jnp.concatenate((got, other), axis=0)
    down_out = maps[:, :, :out_part]
    up_out = maps[:, :, out_part : 2 * out_part].reshape(-1, out_part)
    up_qkv = maps[:, :, 2 * out_part :].reshape(-1, qkv_part)
    row_mask = store_row[:, None] == row_ids[None, :]

    own = jnp.arange(owned, dtype=jnp.int32) + t * owned
    own_ids = jnp.concatenate((first + own, second + own))
    own_mask = store_row[:, None] == own_ids[None, :]

    def pick(products, mask):
        shaped = products.reshape(tok_rows, mask.shape[1], rank)
        return jnp.sum(jnp.where(mask[:, :, None], shaped, 0.0), axis=1)

    a_two = jnp.concatenate((a_qkv, a_other), axis=0)
    low_a = jnp.einsum("td,rdk->trk", hidden, a_two, preferred_element_type=f32)
    low_b = jnp.einsum("td,rkd->trk", context, down_out, preferred_element_type=f32)
    low_qkv, low_out = lax.psum((pick(low_a, own_mask), pick(low_b, row_mask)), "tensor")

    def expand(low, up_maps):
        spread = jnp.where(row_mask[:, :, None], low.astype(bf16)[:, None, :], jnp.zeros((), bf16))
        return jnp.dot(spread.reshape(tok_rows, -1), up_maps, preferred_element_type=f32)

    base_qkv = jnp.dot(hidden, w_qkv, preferred_element_type=f32)
    qkv = (base_qkv + expand(low_qkv, up_qkv)).astype(bf16)
    attn_out = (base_out + expand(low_out, up_out)).astype(bf16)
    return (qkv, attn_out)


def solution(mesh):
    placed = (
        P(("groups", "dp"), None),
        P(("groups", "dp"), "tensor"),
        P(None, "tensor"),
        P("tensor", None),
        P(("dp", "tensor"), None, None),
        P(("dp", "tensor"), None, None),
        P(("dp", "tensor"), None, None),
        P(("dp", "tensor"), None, None),
        P(("groups", "dp"), None),
        P(("groups", "dp"), None),
        P("groups", None),
        P(),
    )
    return jax.shard_map(
        shards,
        mesh=mesh,
        in_specs=placed,
        out_specs=(P(("groups", "dp"), "tensor"), P(("groups", "dp"), "tensor")),
        check_vma=False,
    )
```

```python
import jax
import jax.numpy as jnp
from jax import lax
from jax.sharding import PartitionSpec as P


def chunk_order(depth):
    rows = []
    for z in range(depth):
        row = []
        for s in range(depth - 1):
            for d, ok in ((z + depth - 1 - s, s >= z), (z - depth + 1 + s, s >= depth - 1 - z)):
                if ok:
                    row.append(d)
        rows.append(row + [z])
    return rows


def token_rows(seg_len, seg_use, row_of_use, tok_rows):
    count = seg_len.shape[0]
    order = jnp.arange(count, dtype=jnp.int32)
    ends = jnp.sum(jnp.where(order[None, :] <= order[:, None], seg_len[None, :], 0), axis=1)
    used = jnp.arange(row_of_use.shape[0], dtype=jnp.int32)
    seg_row = jnp.sum(jnp.where(seg_use[:, None] == used[None, :], row_of_use[None, :], 0), axis=1)
    positions = jnp.arange(tok_rows, dtype=jnp.int32)
    inside = (positions[:, None] >= (ends - seg_len)[None, :]) & (positions[:, None] < ends[None, :])
    return jnp.sum(jnp.where(inside, seg_row[None, :], 0), axis=1)


def shards(
    hidden,
    context,
    w_qkv,
    w_out,
    a_qkv,
    b_qkv,
    a_out,
    b_out,
    seg_len,
    seg_use,
    used_list,
    adapter_slot,
):
    f32, bf16 = jnp.float32, jnp.bfloat16
    tensor_size = lax.axis_size("tensor")
    dp_size = lax.axis_size("dp")
    t = lax.axis_index("tensor")
    dp_rank = lax.axis_index("dp")
    tok_rows, model_width = hidden.shape
    owned, _, rank = a_qkv.shape
    out_part = model_width // tensor_size
    qkv_part = b_qkv.shape[2] // tensor_size
    depth = tensor_size // 2
    z, y = t // 2, t % 2

    used = used_list[dp_rank][:, None] == jnp.arange(adapter_slot.shape[0], dtype=jnp.int32)[None, :]
    row_of_use = jnp.sum(jnp.where(used, adapter_slot[None, :], 0), axis=1)
    store_row = token_rows(seg_len[0], seg_use[0], row_of_use, tok_rows)

    order = jnp.asarray(chunk_order(depth), jnp.int32)[z]
    swap = [(i, i ^ 1) for i in range(tensor_size)]
    both = [(0, 1), (1, 0)]
    barrier = lax.optimization_barrier

    row_half = out_part // dp_size
    my_rows = lax.dynamic_slice_in_dim(w_out, dp_rank * row_half, row_half, 0)

    def cols(weights, d, side):
        return lax.dynamic_slice_in_dim(weights, (2 * d + side) * out_part, out_part, 1)

    def trade(pieces):
        sent = jnp.concatenate([cols(my_rows, order[k], 1 - y) for k in pieces], axis=1)
        mine = lax.ppermute(sent, "tensor", swap)
        other = lax.ppermute(mine, "dp", both)
        return jnp.concatenate(
            (jnp.where(dp_rank == 0, mine, other), jnp.where(dp_rank == 0, other, mine)), axis=0
        )

    context_two = jnp.concatenate((context, lax.ppermute(context, "tensor", swap)), axis=1)
    w_first = trade([0])
    w_rest = trade(list(range(1, depth)))

    def reduced_chunk(k):
        theirs = w_first if k == 0 else w_rest[:, (k - 1) * out_part : k * out_part]
        weights = jnp.concatenate((cols(w_out, order[k], y), theirs), axis=0)
        return jnp.dot(context_two, weights, preferred_element_type=f32)

    def split(maps, part):
        return jnp.transpose(maps.reshape(owned, rank, tensor_size, part), (2, 0, 1, 3))

    def spread_rows(sent):
        got = lax.all_to_all(sent, "tensor", split_axis=0, concat_axis=0, tiled=True)
        got = got.reshape((-1,) + got.shape[2:])
        return jnp.concatenate((got, lax.ppermute(got, "dp", both)), axis=0)

    a_other = lax.ppermute(a_qkv, "dp", both)
    down_out = spread_rows(split(jnp.transpose(a_out, (0, 2, 1)), out_part))
    up_sent = jnp.concatenate((split(b_out, out_part), split(b_qkv, qkv_part)), axis=3)
    up_maps = spread_rows(up_sent)
    up_out = up_maps[:, :, :out_part].reshape(-1, out_part)
    up_qkv = up_maps[:, :, out_part:].reshape(-1, qkv_part)

    half = tensor_size * owned
    first, second = dp_rank * half, (1 - dp_rank) * half

    def lane_mask(rows):
        return store_row[:, None] == jnp.repeat(rows, rank)[None, :]

    rows = jnp.arange(half, dtype=jnp.int32)
    row_mask = lane_mask(jnp.concatenate((first + rows, second + rows)))
    own = jnp.arange(owned, dtype=jnp.int32) + t * owned
    own_mask = lane_mask(jnp.concatenate((first + own, second + own)))

    def pick(products, mask):
        kept = jnp.where(mask, products, 0.0)
        wide = sum(kept[:, i : i + 2 * rank] for i in range(0, kept.shape[1], 2 * rank))
        return wide[:, :rank] + wide[:, rank:]

    a_two = jnp.concatenate((a_qkv, a_other), axis=0)
    low_a = pick(
        jnp.dot(hidden, jnp.transpose(a_two, (1, 0, 2)).reshape(model_width, -1), preferred_element_type=f32),
        own_mask,
    )
    low_b = pick(
        lax.dot_general(
            context,
            down_out.reshape(-1, out_part),
            (((1,), (1,)), ((), ())),
            preferred_element_type=f32,
        ),
        row_mask,
    )
    low = jnp.concatenate((low_a, low_b), axis=1)
    step = 1
    while step < tensor_size:
        pairs = [(i, i ^ step) for i in range(tensor_size)]
        low = low + lax.ppermute(low.astype(bf16), "tensor", pairs).astype(f32)
        step = 2 * step
    low = low.astype(bf16)

    def expand(low_rank, maps):
        twice = jnp.concatenate((low_rank, low_rank), axis=1)
        spread = jnp.concatenate([twice] * (row_mask.shape[1] // (2 * rank)), axis=1)
        spread = jnp.where(row_mask, spread, jnp.zeros((), bf16))
        return jnp.dot(spread, maps, preferred_element_type=f32)

    reduced, up, down, late = [], None, None, hidden

    def chosen(d):
        value = reduced[0]
        for k in range(1, len(reduced)):
            value = jnp.where(order[k] == d, reduced[k], value)
        return value

    for s in range(depth - 1):
        reduced.append(reduced_chunk(s))
        to_up, to_down = chosen(z + depth - 1 - s), chosen(z - depth + 1 + s)
        if s > 0:
            to_up, to_down = to_up + up.astype(f32), to_down + down.astype(f32)
        to_up, to_down = to_up.astype(bf16), to_down.astype(bf16)
        if s == 0:
            to_up, to_down, late = barrier((to_up, to_down, late))
        up_pairs = [(2 * i + j, 2 * i + 2 + j) for i in range(s + 1) for j in range(2)]
        down_pairs = [
            (2 * i + j, 2 * i - 2 + j) for i in range(depth - 1 - s, depth) for j in range(2)
        ]
        up = lax.ppermute(to_up, "tensor", up_pairs)
        down = lax.ppermute(to_down, "tensor", down_pairs)

    base_qkv = jnp.dot(late, w_qkv, preferred_element_type=f32)
    qkv = (base_qkv + expand(low[:, :rank], up_qkv)).astype(bf16)
    here = reduced_chunk(depth - 1) + expand(low[:, rank:], up_out)
    qkv, here = barrier((qkv, here))
    attn_out = (here + up.astype(f32) + down.astype(f32)).astype(bf16)
    return (qkv, attn_out)


def solution(mesh):
    placed = (
        P(("groups", "dp"), None),
        P(("groups", "dp"), "tensor"),
        P(None, "tensor"),
        P("tensor", None),
        P(("dp", "tensor"), None, None),
        P(("dp", "tensor"), None, None),
        P(("dp", "tensor"), None, None),
        P(("dp", "tensor"), None, None),
        P(("groups", "dp"), None),
        P(("groups", "dp"), None),
        P("groups", None),
        P(),
    )
    return jax.shard_map(
        shards,
        mesh=mesh,
        in_specs=placed,
        out_specs=(P(("groups", "dp"), "tensor"), P(("groups", "dp"), "tensor")),
        check_vma=False,
    )
```

```python
import functools

import jax
import jax.numpy as jnp
from jax import lax
from jax.experimental import pallas as pl
from jax.experimental.pallas import tpu as pltpu
from jax.sharding import PartitionSpec as P

MESH = pl.DeviceIdType.MESH


def project(
    tensor_size,
    hidden_hbm,
    w_qkv_hbm,
    context,
    w_out,
    maps,
    a_own,
    store_row,
    base_qkv,
    base_out,
    got,
    low,
    hidden,
    w_qkv,
    context_two,
    w_two,
    going,
    above,
    below,
    a_two,
    low_part,
    low_in,
    load_sem,
    pair_send,
    pair_recv,
    w_send,
    w_recv,
    line_send,
    up_recv,
    down_recv,
    maps_send,
    maps_recv,
    core_send,
    core_recv,
    hand_send,
    hand_recv,
    a_send,
    a_recv,
    low_send,
    low_recv,
    share_send,
    share_recv,
):
    f32, bf16 = jnp.float32, jnp.bfloat16
    group, core, t = lax.axis_index("groups"), lax.axis_index("dp"), lax.axis_index("tensor")
    depth = tensor_size // 2
    z, y = t // 2, t % 2
    rows, part = context.shape
    last = depth - 1

    def device(core_of, tensor_of):
        return (group, core_of, tensor_of)

    pair = device(core, 2 * z + 1 - y)
    twin = device(1 - core, t)
    peers = [lax.rem(t + i, tensor_size) for i in range(1, tensor_size)]

    loads = [
        pltpu.make_async_copy(w_qkv_hbm, w_qkv, load_sem.at[0]),
        pltpu.make_async_copy(hidden_hbm, hidden, load_sem.at[1]),
    ]
    for load in loads:
        load.start()

    barrier = pltpu.get_barrier_semaphore()
    for peer in peers:
        pl.semaphore_signal(barrier, inc=1, device_id=device(core, peer), device_id_type=MESH)
    pl.semaphore_signal(barrier, inc=1, device_id=twin, device_id_type=MESH)
    pl.semaphore_wait(barrier, tensor_size)

    def remote(src, dst, send, recv, to):
        return pltpu.make_async_remote_copy(
            src_ref=src, dst_ref=dst, send_sem=send, recv_sem=recv, device_id=to, device_id_type=MESH
        )

    half_rows = rows // 2
    halves = [pl.ds(h * half_rows, half_rows) for h in range(2)]

    def trade(h):
        return remote(context.at[halves[h]], context_two.at[halves[h]], pair_send.at[h], pair_recv.at[h], pair)

    core_rows = pl.ds(pl.multiple_of(core * (part // 2), 16), part // 2)

    def weights(d):
        their_cols = pl.ds(pl.multiple_of((2 * d + 1 - y) * part, 128), part)
        return remote(w_out.at[core_rows, their_cols], w_two.at[d, core_rows], w_send.at[d], w_recv.at[d], pair)

    def hand(d):
        return remote(w_two.at[d, core_rows], w_two.at[d, core_rows], hand_send.at[d], hand_recv.at[d], twin)

    def hand_on(d, up, s):
        weights(d).wait_recv()
        hand(d).start()

    rank = maps.shape[0] // tensor_size

    def map_rows(source):
        return pl.ds(pl.multiple_of(source * rank, 16), rank)

    def map_copy(i):
        src, dst = maps.at[map_rows(peers[i])], got.at[0, map_rows(t)]
        return remote(src, dst, maps_send.at[i], maps_recv.at[i], device(core, peers[i]))

    def pass_on(i):
        source = lax.rem(t + tensor_size - 1 - i, tensor_size)
        src, dst = got.at[0, map_rows(source)], got.at[1, map_rows(source)]
        return remote(src, dst, core_send.at[i], core_recv.at[i], twin)

    a_copy = remote(a_own, a_two.at[pl.ds(rank, rank)], a_send, a_recv, twin)
    share_rows = rows // tensor_size

    def rows_of(device_index):
        return pl.ds(pl.multiple_of(device_index * share_rows, 16), share_rows)

    def low_copy(i):
        to = device(core, peers[i])
        return remote(low_part.at[rows_of(peers[i])], low_in.at[i], low_send.at[i], low_recv.at[i], to)

    def share(i):
        to = device(core, peers[i])
        return remote(low.at[rows_of(t)], low.at[rows_of(t)], share_send.at[i], share_recv.at[i], to)

    def each(s, act):
        if s == last:
            act(z, None, s)
            return

        @pl.when(z <= s)
        def _():
            act(z + last - s, True, s)

        @pl.when(z >= last - s)
        def _():
            act(z - last + s, False, s)

    def chunk(d, tile):
        cols = pl.ds(pl.multiple_of((2 * d + y) * part, 128), part)
        own = jnp.dot(context[tile, :], w_out[:, cols], preferred_element_type=f32)
        return own + jnp.dot(context_two[tile, :], w_two[d], preferred_element_type=f32)

    def line_copy(d, up, s, h):
        slot = above if up else below
        recv = up_recv if up else down_recv
        to = device(core, lax.rem(t + (2 if up else tensor_size - 2), tensor_size))
        src, dst = going.at[d, halves[h]], slot.at[s, halves[h]]
        return remote(src, dst, line_send.at[d, h], recv.at[s, h], to)

    tile_rows = min(half_rows, 256)
    tiles = rows // tile_rows
    half_tiles = half_rows // tile_rows

    def tile_of(i):
        return pl.ds(pl.multiple_of(i * tile_rows, tile_rows), tile_rows)

    def over(count, start, body):
        def step(i, carry):
            body(tile_of(start + i))
            return carry

        lax.fori_loop(0, count, step, 0)

    def send(d, up, s, h):
        if h == 0:
            hand(d).wait_recv()

        def first(tile):
            base_out[tile, :] = chunk(d, tile)

        def plain(tile):
            going[d, tile, :] = base_out[tile, :].astype(bf16)

        def added(tile):
            came = (above if up else below)[s - 1, tile, :].astype(f32)
            going[d, tile, :] = (base_out[tile, :] + came).astype(bf16)

        over(half_tiles, h * half_tiles, first)
        if s == 0:
            over(half_tiles, h * half_tiles, plain)
        else:
            inner = z > 0 if up else z < last

            @pl.when(inner)
            def _():
                line_copy(d, up, s - 1, h).wait_recv()
                over(half_tiles, h * half_tiles, added)

            @pl.when(jnp.logical_not(inner))
            def _():
                over(half_tiles, h * half_tiles, plain)

        line_copy(d, up, s, h).start()

    each(0, lambda d, up, s: weights(d).start())
    trade(0).start()
    for i in range(tensor_size - 1):
        map_copy(i).start()
    own_maps = remote(
        maps.at[map_rows(t)],
        got.at[1, map_rows(t)],
        core_send.at[tensor_size - 1],
        core_recv.at[tensor_size - 1],
        twin,
    )
    own_maps.start()
    a_copy.start()
    got[0, map_rows(t)] = maps[map_rows(t)]
    a_two[:rank] = a_own[...]
    each(0, hand_on)
    trade(0).wait_recv()
    trade(1).start()
    each(0, functools.partial(send, h=0))
    trade(1).wait_recv()
    each(1, lambda d, up, s: weights(d).start())
    each(0, functools.partial(send, h=1))

    for load in loads:
        load.wait()
    a_copy.wait()
    lanes = lax.broadcasted_iota(jnp.int32, (tile_rows, 2 * rank), 1)
    own_id = jnp.where(lanes < rank, core, 1 - core) * tensor_size + t

    def joined(tile):
        base_qkv[tile, :] = jnp.dot(hidden[tile, :], w_qkv[...], preferred_element_type=f32)
        down = lax.dot_general(
            hidden[tile, :], a_two[...], (((1,), (1,)), ((), ())), preferred_element_type=f32
        )
        down = jnp.where(store_row[tile, :] == own_id, down, 0.0)
        low_part[tile, :] = down + pltpu.roll(down, rank, 1)

    def low_out(tile):
        total = jnp.zeros((tile_rows, 2 * rank), f32)
        for c in range(2):
            down = lax.dot_general(
                context[tile, :], got[c, :, :part], (((1,), (1,)), ((), ())), preferred_element_type=f32
            )
            first = (core if c == 0 else 1 - core) * tensor_size
            for j in range(tensor_size // 2):
                ids = first + 2 * j + jnp.where(lanes < rank, 0, 1)
                cut = down[:, 2 * rank * j : 2 * rank * (j + 1)]
                total = total + jnp.where(store_row[tile, :] == ids, cut, 0.0)
        total = total + pltpu.roll(total, rank, 1)
        low_part[tile, :] = jnp.where(lanes < rank, low_part[tile, :], total)

    over(tiles, 0, joined)
    for s in range(1, last):
        each(s, hand_on)
        each(s + 1, lambda d, up, s: weights(d).start())
        for h in range(2):
            each(s, functools.partial(send, h=h))
        if s == 1:
            for i in range(tensor_size - 1):
                map_copy(i).wait_recv()
                pass_on(i).start()
    each(last, hand_on)

    for i in range(tensor_size - 1):
        pass_on(i).wait()
        map_copy(i).wait_send()
    own_maps.wait()
    over(tiles, 0, low_out)
    for i in range(tensor_size - 1):
        low_copy(i).start()
    hand(z).wait_recv()

    def own(tile):
        base_out[tile, :] = chunk(z, tile)

    over(tiles, 0, own)
    whole = low_part[rows_of(t)]
    for i in range(tensor_size - 1):
        low_copy(i).wait_recv()
        whole = whole + low_in[i]
    low[rows_of(t)] = whole.astype(bf16)
    for i in range(tensor_size - 1):
        share(i).start()

    for h in range(2):
        for up in (True, False):

            @pl.when(z > 0 if up else z < last)
            def _():
                line_copy(z, up, last - 1, h).wait_recv()

                def added(tile):
                    came = (above if up else below)[last - 1, tile, :].astype(f32)
                    base_out[tile, :] = base_out[tile, :] + came

                over(half_tiles, h * half_tiles, added)

    for i in range(tensor_size - 1):
        share(i).wait()
        low_copy(i).wait_send()
    for s in range(depth):
        each(s, lambda d, up, s: (weights(d).wait_send(), hand(d).wait_send()))
    for h in range(2):
        trade(h).wait_send()
        for s in range(last):
            each(s, lambda d, up, s: line_copy(d, up, s, h).wait_send())


def projections(tensor_size, hidden, w_qkv, context, w_out, maps, a_own, store_row):
    f32, bf16 = jnp.float32, jnp.bfloat16
    rows, part = context.shape
    depth, rank = tensor_size // 2, a_own.shape[0]
    in_vmem = pl.BlockSpec(memory_space=pltpu.VMEM)
    in_hbm = pl.BlockSpec(memory_space=pl.ANY)
    dma = pltpu.SemaphoreType.DMA
    return pl.pallas_call(
        functools.partial(project, tensor_size),
        out_shape=(
            jax.ShapeDtypeStruct((rows, w_qkv.shape[1]), f32),
            jax.ShapeDtypeStruct((rows, part), f32),
            jax.ShapeDtypeStruct((2,) + maps.shape, bf16),
            jax.ShapeDtypeStruct((rows, 2 * rank), bf16),
        ),
        in_specs=[in_hbm, in_hbm] + [in_vmem] * 5,
        out_specs=(in_vmem,) * 4,
        scratch_shapes=[
            pltpu.VMEM(hidden.shape, bf16),
            pltpu.VMEM(w_qkv.shape, bf16),
            pltpu.VMEM(context.shape, bf16),
            pltpu.VMEM((depth, part, part), bf16),
            pltpu.VMEM((depth, rows, part), bf16),
            pltpu.VMEM((depth - 1, rows, part), bf16),
            pltpu.VMEM((depth - 1, rows, part), bf16),
            pltpu.VMEM((2 * rank, hidden.shape[1]), bf16),
            pltpu.VMEM((rows, 2 * rank), f32),
            pltpu.VMEM((tensor_size - 1, rows // tensor_size, 2 * rank), f32),
            dma((2,)),
            dma((2,)),
            dma((2,)),
            dma((depth,)),
            dma((depth,)),
            dma((depth, 2)),
            dma((depth - 1, 2)),
            dma((depth - 1, 2)),
            dma((tensor_size - 1,)),
            dma((tensor_size - 1,)),
            dma((tensor_size,)),
            dma((tensor_size,)),
            dma((depth,)),
            dma((depth,)),
            dma(()),
            dma(()),
        ]
        + [dma((tensor_size - 1,))] * 4,
        compiler_params=pltpu.CompilerParams(
            collective_id=0, has_side_effects=True, vmem_limit_bytes=62 * 1024 * 1024
        ),
        cost_estimate=pl.CostEstimate(
            flops=2 * rows * (hidden.shape[1] * w_qkv.shape[1] + 2 * part * part * depth),
            bytes_accessed=2 * (hidden.size + w_qkv.size + w_out.size + context.size),
            transcendentals=0,
        ),
    )(hidden, w_qkv, context, w_out, maps, a_own, store_row)


def chunk_order(depth):
    rows = []
    for z in range(depth):
        row = []
        for s in range(depth - 1):
            for d, ok in ((z + depth - 1 - s, s >= z), (z - depth + 1 + s, s >= depth - 1 - z)):
                if ok:
                    row.append(d)
        rows.append(row + [z])
    return rows


def token_rows(seg_len, seg_use, row_of_use, tok_rows):
    count = seg_len.shape[0]
    order = jnp.arange(count, dtype=jnp.int32)
    ends = jnp.sum(jnp.where(order[None, :] <= order[:, None], seg_len[None, :], 0), axis=1)
    used = jnp.arange(row_of_use.shape[0], dtype=jnp.int32)
    seg_row = jnp.sum(jnp.where(seg_use[:, None] == used[None, :], row_of_use[None, :], 0), axis=1)
    positions = jnp.arange(tok_rows, dtype=jnp.int32)
    inside = (positions[:, None] >= (ends - seg_len)[None, :]) & (positions[:, None] < ends[None, :])
    return jnp.sum(jnp.where(inside, seg_row[None, :], 0), axis=1)


def plain_shards(
    hidden,
    context,
    w_qkv,
    w_out,
    a_qkv,
    b_qkv,
    a_out,
    b_out,
    seg_len,
    seg_use,
    used_list,
    adapter_slot,
):
    f32, bf16 = jnp.float32, jnp.bfloat16
    tensor_size = lax.axis_size("tensor")
    dp_size = lax.axis_size("dp")
    t = lax.axis_index("tensor")
    dp_rank = lax.axis_index("dp")
    tok_rows, model_width = hidden.shape
    owned, _, rank = a_qkv.shape
    out_part = model_width // tensor_size
    qkv_part = b_qkv.shape[2] // tensor_size
    depth = tensor_size // 2
    z, y = t // 2, t % 2

    used = used_list[dp_rank][:, None] == jnp.arange(adapter_slot.shape[0], dtype=jnp.int32)[None, :]
    row_of_use = jnp.sum(jnp.where(used, adapter_slot[None, :], 0), axis=1)
    store_row = token_rows(seg_len[0], seg_use[0], row_of_use, tok_rows)

    def out_cols(d, side):
        return lax.dynamic_slice_in_dim(w_out, (2 * d + side) * out_part, out_part, 1)

    def partial(d, side):
        return jnp.dot(context, out_cols(d, side), preferred_element_type=f32)

    order = jnp.asarray(chunk_order(depth), jnp.int32)[z]
    swap = [(i, i ^ 1) for i in range(tensor_size)]
    both = [(0, 1), (1, 0)]

    def split(maps, part):
        return jnp.transpose(maps.reshape(owned, rank, tensor_size, part), (2, 0, 1, 3))

    a_out_t = jnp.transpose(a_out, (0, 2, 1))
    sent = jnp.concatenate(
        (split(a_out_t, out_part), split(b_out, out_part), split(b_qkv, qkv_part)), axis=3
    )

    reduced, up, down = [], None, None

    def chosen(d):
        value = reduced[0]
        for k in range(1, len(reduced)):
            value = jnp.where(order[k] == d, reduced[k], value)
        return value

    for k in range(depth):
        mine = lax.ppermute(partial(order[k], 1 - y).astype(bf16), "tensor", swap)
        reduced.append(mine.astype(f32) + partial(order[k], y))
        if k < depth - 1:
            s = k
            outgoing_up = chosen(z + depth - 1 - s)
            outgoing_down = chosen(z - depth + 1 + s)
            if s > 0:
                outgoing_up = outgoing_up + up.astype(f32)
                outgoing_down = outgoing_down + down.astype(f32)
            up_pairs = [(2 * i + j, 2 * i + 2 + j) for i in range(s + 1) for j in range(2)]
            down_pairs = [
                (2 * i + j, 2 * i - 2 + j) for i in range(depth - 1 - s, depth) for j in range(2)
            ]
            up = lax.ppermute(outgoing_up.astype(bf16), "tensor", up_pairs)
            down = lax.ppermute(outgoing_down.astype(bf16), "tensor", down_pairs)
        if k == 0:
            got = lax.all_to_all(sent, "tensor", split_axis=0, concat_axis=0, tiled=True)
            got = got.reshape((tensor_size * owned,) + got.shape[2:])
            other = lax.ppermute(got, "dp", both)
            a_other = lax.ppermute(a_qkv, "dp", both)
    base_out = reduced[-1] + up.astype(f32) + down.astype(f32)

    half = tensor_size * owned
    first = dp_rank * half
    second = (1 - dp_rank) * half
    rows = jnp.arange(half, dtype=jnp.int32)
    row_ids = jnp.concatenate((first + rows, second + rows))
    maps = jnp.concatenate((got, other), axis=0)
    down_out = maps[:, :, :out_part]
    up_out = maps[:, :, out_part : 2 * out_part].reshape(-1, out_part)
    up_qkv = maps[:, :, 2 * out_part :].reshape(-1, qkv_part)
    row_mask = store_row[:, None] == row_ids[None, :]

    own = jnp.arange(owned, dtype=jnp.int32) + t * owned
    own_ids = jnp.concatenate((first + own, second + own))
    own_mask = store_row[:, None] == own_ids[None, :]

    def pick(products, mask):
        shaped = products.reshape(tok_rows, mask.shape[1], rank)
        return jnp.sum(jnp.where(mask[:, :, None], shaped, 0.0), axis=1)

    a_two = jnp.concatenate((a_qkv, a_other), axis=0)
    low_a = jnp.einsum("td,rdk->trk", hidden, a_two, preferred_element_type=f32)
    low_b = jnp.einsum("td,rkd->trk", context, down_out, preferred_element_type=f32)
    low_qkv, low_out = lax.psum((pick(low_a, own_mask), pick(low_b, row_mask)), "tensor")

    def expand(low, up_maps):
        spread = jnp.where(row_mask[:, :, None], low.astype(bf16)[:, None, :], jnp.zeros((), bf16))
        return jnp.dot(spread.reshape(tok_rows, -1), up_maps, preferred_element_type=f32)

    base_qkv = jnp.dot(hidden, w_qkv, preferred_element_type=f32)
    qkv = (base_qkv + expand(low_qkv, up_qkv)).astype(bf16)
    attn_out = (base_out + expand(low_out, up_out)).astype(bf16)
    return (qkv, attn_out)


def shards(
    hidden,
    context,
    w_qkv,
    w_out,
    a_qkv,
    b_qkv,
    a_out,
    b_out,
    seg_len,
    seg_use,
    used_list,
    adapter_slot,
):
    f32, bf16 = jnp.float32, jnp.bfloat16
    tensor_size = lax.axis_size("tensor")
    dp_size = lax.axis_size("dp")
    t = lax.axis_index("tensor")
    dp_rank = lax.axis_index("dp")
    tok_rows, model_width = hidden.shape
    owned, _, rank = a_qkv.shape
    out_part = model_width // tensor_size
    qkv_part = b_qkv.shape[2] // tensor_size
    if tensor_size % 2 or tensor_size < 6 or out_part % 128 or qkv_part % 128 or owned != 1 or rank != 64 or tok_rows % 512:
        return plain_shards(
            hidden, context, w_qkv, w_out, a_qkv, b_qkv, a_out, b_out,
            seg_len, seg_use, used_list, adapter_slot,
        )

    used = used_list[dp_rank][:, None] == jnp.arange(adapter_slot.shape[0], dtype=jnp.int32)[None, :]
    row_of_use = jnp.sum(jnp.where(used, adapter_slot[None, :], 0), axis=1)
    store_row = token_rows(seg_len[0], seg_use[0], row_of_use, tok_rows)

    def split(maps, part):
        return jnp.transpose(maps.reshape(rank, tensor_size, part), (1, 0, 2))

    sent = jnp.concatenate(
        (
            split(jnp.transpose(a_out, (0, 2, 1)), out_part),
            split(b_out, out_part),
            split(b_qkv, qkv_part),
        ),
        axis=2,
    )
    sent = sent.reshape(-1, sent.shape[2])
    store_lanes = jnp.broadcast_to(store_row[:, None], (tok_rows, 2 * rank))
    base_qkv, base_out, got, low = projections(
        tensor_size, hidden, w_qkv, context, w_out, sent, jnp.transpose(a_qkv[0]), store_lanes
    )
    got = got.reshape(-1, got.shape[2])
    up_out = got[:, out_part : 2 * out_part]
    up_qkv = got[:, 2 * out_part :]

    half = tensor_size * owned
    first, second = dp_rank * half, (1 - dp_rank) * half

    def lane_mask(rows):
        return store_row[:, None] == jnp.repeat(rows, rank)[None, :]

    rows = jnp.arange(half, dtype=jnp.int32)
    row_mask = lane_mask(jnp.concatenate((first + rows, second + rows)))

    def expand(start, maps):
        lanes = jnp.arange(row_mask.shape[1], dtype=jnp.int32) % rank + start
        copies = (jnp.arange(2 * rank, dtype=jnp.int32)[:, None] == lanes[None, :]).astype(bf16)
        spread = jnp.dot(low, copies, preferred_element_type=f32).astype(bf16)
        spread = jnp.where(row_mask, spread, jnp.zeros((), bf16))
        return jnp.dot(spread, maps, preferred_element_type=f32)

    qkv = (base_qkv + expand(0, up_qkv)).astype(bf16)
    attn_out = (base_out + expand(rank, up_out)).astype(bf16)
    return (qkv, attn_out)


def solution(mesh):
    placed = (
        P(("groups", "dp"), None),
        P(("groups", "dp"), "tensor"),
        P(None, "tensor"),
        P("tensor", None),
        P(("dp", "tensor"), None, None),
        P(("dp", "tensor"), None, None),
        P(("dp", "tensor"), None, None),
        P(("dp", "tensor"), None, None),
        P(("groups", "dp"), None),
        P(("groups", "dp"), None),
        P("groups", None),
        P(),
    )
    return jax.shard_map(
        shards,
        mesh=mesh,
        in_specs=placed,
        out_specs=(P(("groups", "dp"), "tensor"), P(("groups", "dp"), "tensor")),
        check_vma=False,
    )
```

```python
import functools

import jax
import jax.numpy as jnp
from jax import lax
from jax.experimental import pallas as pl
from jax.experimental.pallas import tpu as pltpu
from jax.sharding import PartitionSpec as P

MESH = pl.DeviceIdType.MESH


def project(
    tensor_size,
    hidden_hbm,
    w_qkv_hbm,
    context,
    w_out,
    maps,
    a_own,
    store_row,
    base_qkv,
    base_out,
    got,
    low,
    hidden,
    w_qkv,
    context_two,
    w_two,
    going,
    above,
    below,
    a_two,
    low_part,
    low_in,
    load_sem,
    pair_send,
    pair_recv,
    w_send,
    w_recv,
    line_send,
    up_recv,
    down_recv,
    maps_send,
    maps_recv,
    core_send,
    core_recv,
    hand_send,
    hand_recv,
    a_send,
    a_recv,
    low_send,
    low_recv,
    share_send,
    share_recv,
):
    f32, bf16 = jnp.float32, jnp.bfloat16
    group, core, t = lax.axis_index("groups"), lax.axis_index("dp"), lax.axis_index("tensor")
    depth = tensor_size // 2
    z, y = t // 2, t % 2
    rows, part = context.shape
    last = depth - 1

    def device(core_of, tensor_of):
        return (group, core_of, tensor_of)

    pair = device(core, 2 * z + 1 - y)
    twin = device(1 - core, t)
    peers = [lax.rem(t + i, tensor_size) for i in range(1, tensor_size)]

    loads = [
        pltpu.make_async_copy(w_qkv_hbm, w_qkv, load_sem.at[0]),
        pltpu.make_async_copy(hidden_hbm, hidden, load_sem.at[1]),
    ]
    for load in loads:
        load.start()

    barrier = pltpu.get_barrier_semaphore()
    for peer in peers:
        pl.semaphore_signal(barrier, inc=1, device_id=device(core, peer), device_id_type=MESH)
    pl.semaphore_signal(barrier, inc=1, device_id=twin, device_id_type=MESH)
    pl.semaphore_wait(barrier, tensor_size)

    def remote(src, dst, send, recv, to):
        return pltpu.make_async_remote_copy(
            src_ref=src, dst_ref=dst, send_sem=send, recv_sem=recv, device_id=to, device_id_type=MESH
        )

    half_rows = rows // 2
    halves = [pl.ds(h * half_rows, half_rows) for h in range(2)]

    def trade(h):
        return remote(context.at[halves[h]], context_two.at[halves[h]], pair_send.at[h], pair_recv.at[h], pair)

    core_rows = pl.ds(pl.multiple_of(core * (part // 2), 16), part // 2)

    def weights(d):
        their_cols = pl.ds(pl.multiple_of((2 * d + 1 - y) * part, 128), part)
        return remote(w_out.at[core_rows, their_cols], w_two.at[d, core_rows], w_send.at[d], w_recv.at[d], pair)

    def hand(d):
        return remote(w_two.at[d, core_rows], w_two.at[d, core_rows], hand_send.at[d], hand_recv.at[d], twin)

    def hand_on(d, up, s):
        weights(d).wait_recv()
        hand(d).start()

    rank = maps.shape[0] // tensor_size

    def map_rows(source):
        return pl.ds(pl.multiple_of(source * rank, 16), rank)

    def map_copy(i):
        src, dst = maps.at[map_rows(peers[i])], got.at[0, map_rows(t)]
        return remote(src, dst, maps_send.at[i], maps_recv.at[i], device(core, peers[i]))

    def pass_on(i):
        source = lax.rem(t + tensor_size - 1 - i, tensor_size)
        src, dst = got.at[0, map_rows(source)], got.at[1, map_rows(source)]
        return remote(src, dst, core_send.at[i], core_recv.at[i], twin)

    a_copy = remote(a_own, a_two.at[pl.ds(rank, rank)], a_send, a_recv, twin)
    share_rows = rows // tensor_size

    def rows_of(device_index):
        return pl.ds(pl.multiple_of(device_index * share_rows, 16), share_rows)

    def low_copy(i):
        to = device(core, peers[i])
        return remote(low_part.at[rows_of(peers[i])], low_in.at[i], low_send.at[i], low_recv.at[i], to)

    def share(i):
        to = device(core, peers[i])
        return remote(low.at[rows_of(t)], low.at[rows_of(t)], share_send.at[i], share_recv.at[i], to)

    def each(s, act):
        if s == last:
            act(z, None, s)
            return

        @pl.when(z <= s)
        def _():
            act(z + last - s, True, s)

        @pl.when(z >= last - s)
        def _():
            act(z - last + s, False, s)

    def chunk(d, tile):
        cols = pl.ds(pl.multiple_of((2 * d + y) * part, 128), part)
        own = jnp.dot(context[tile, :], w_out[:, cols], preferred_element_type=f32)
        return own + jnp.dot(context_two[tile, :], w_two[d], preferred_element_type=f32)

    def line_copy(d, up, s, h):
        slot = above if up else below
        recv = up_recv if up else down_recv
        to = device(core, lax.rem(t + (2 if up else tensor_size - 2), tensor_size))
        src, dst = going.at[d, halves[h]], slot.at[s, halves[h]]
        return remote(src, dst, line_send.at[d, h], recv.at[s, h], to)

    tile_rows = min(half_rows, 256)
    tiles = rows // tile_rows
    half_tiles = half_rows // tile_rows

    def tile_of(i):
        return pl.ds(pl.multiple_of(i * tile_rows, tile_rows), tile_rows)

    def over(count, start, body):
        def step(i, carry):
            body(tile_of(start + i))
            return carry

        lax.fori_loop(0, count, step, 0)

    def send(d, up, s, h):
        if h == 0:
            hand(d).wait_recv()

        def first(tile):
            base_out[tile, :] = chunk(d, tile)

        def plain(tile):
            going[d, tile, :] = base_out[tile, :].astype(bf16)

        def added(tile):
            came = (above if up else below)[s - 1, tile, :].astype(f32)
            going[d, tile, :] = (base_out[tile, :] + came).astype(bf16)

        over(half_tiles, h * half_tiles, first)
        if s == 0:
            over(half_tiles, h * half_tiles, plain)
        else:
            inner = z > 0 if up else z < last

            @pl.when(inner)
            def _():
                line_copy(d, up, s - 1, h).wait_recv()
                over(half_tiles, h * half_tiles, added)

            @pl.when(jnp.logical_not(inner))
            def _():
                over(half_tiles, h * half_tiles, plain)

        line_copy(d, up, s, h).start()

    each(0, lambda d, up, s: weights(d).start())
    trade(0).start()
    for i in range(tensor_size - 1):
        map_copy(i).start()
    own_maps = remote(
        maps.at[map_rows(t)],
        got.at[1, map_rows(t)],
        core_send.at[tensor_size - 1],
        core_recv.at[tensor_size - 1],
        twin,
    )
    own_maps.start()
    a_copy.start()
    got[0, map_rows(t)] = maps[map_rows(t)]
    a_two[:rank] = a_own[...]
    each(0, hand_on)
    trade(0).wait_recv()
    trade(1).start()
    each(0, functools.partial(send, h=0))
    trade(1).wait_recv()
    for s in range(1, depth):
        each(s, lambda d, up, s: weights(d).start())
    each(0, functools.partial(send, h=1))

    for load in loads:
        load.wait()
    a_copy.wait()
    lanes = lax.broadcasted_iota(jnp.int32, (tile_rows, 2 * rank), 1)
    own_id = jnp.where(lanes < rank, core, 1 - core) * tensor_size + t

    def joined(tile):
        base_qkv[tile, :] = jnp.dot(hidden[tile, :], w_qkv[...], preferred_element_type=f32)
        down = lax.dot_general(
            hidden[tile, :], a_two[...], (((1,), (1,)), ((), ())), preferred_element_type=f32
        )
        down = jnp.where(store_row[tile, :] == own_id, down, 0.0)
        low_part[tile, :] = down + pltpu.roll(down, rank, 1)

    def low_out(tile):
        total = jnp.zeros((tile_rows, 2 * rank), f32)
        for c in range(2):
            down = lax.dot_general(
                context[tile, :], got[c, :, :part], (((1,), (1,)), ((), ())), preferred_element_type=f32
            )
            first = (core if c == 0 else 1 - core) * tensor_size
            for j in range(tensor_size // 2):
                ids = first + 2 * j + jnp.where(lanes < rank, 0, 1)
                cut = down[:, 2 * rank * j : 2 * rank * (j + 1)]
                total = total + jnp.where(store_row[tile, :] == ids, cut, 0.0)
        total = total + pltpu.roll(total, rank, 1)
        low_part[tile, :] = jnp.where(lanes < rank, low_part[tile, :], total)

    over(tiles, 0, joined)
    for s in range(1, depth):
        each(s, hand_on)
    for s in range(1, last):
        for h in range(2):
            each(s, functools.partial(send, h=h))
        if s == 1:
            for i in range(tensor_size - 1):
                map_copy(i).wait_recv()
                pass_on(i).start()

    for i in range(tensor_size - 1):
        pass_on(i).wait()
        map_copy(i).wait_send()
    own_maps.wait()
    over(tiles, 0, low_out)
    for i in range(tensor_size - 1):
        low_copy(i).start()
    hand(z).wait_recv()

    def own(tile):
        base_out[tile, :] = chunk(z, tile)

    over(tiles, 0, own)
    whole = low_part[rows_of(t)]
    for i in range(tensor_size - 1):
        low_copy(i).wait_recv()
        whole = whole + low_in[i]
    low[rows_of(t)] = whole.astype(bf16)
    for i in range(tensor_size - 1):
        share(i).start()

    for h in range(2):
        for up in (True, False):

            @pl.when(z > 0 if up else z < last)
            def _():
                line_copy(z, up, last - 1, h).wait_recv()

                def added(tile):
                    came = (above if up else below)[last - 1, tile, :].astype(f32)
                    base_out[tile, :] = base_out[tile, :] + came

                over(half_tiles, h * half_tiles, added)

    for i in range(tensor_size - 1):
        share(i).wait()
        low_copy(i).wait_send()
    for s in range(depth):
        each(s, lambda d, up, s: (weights(d).wait_send(), hand(d).wait_send()))
    for h in range(2):
        trade(h).wait_send()
        for s in range(last):
            each(s, lambda d, up, s: line_copy(d, up, s, h).wait_send())


def projections(tensor_size, hidden, w_qkv, context, w_out, maps, a_own, store_row):
    f32, bf16 = jnp.float32, jnp.bfloat16
    rows, part = context.shape
    depth, rank = tensor_size // 2, a_own.shape[0]
    in_vmem = pl.BlockSpec(memory_space=pltpu.VMEM)
    in_hbm = pl.BlockSpec(memory_space=pl.ANY)
    dma = pltpu.SemaphoreType.DMA
    return pl.pallas_call(
        functools.partial(project, tensor_size),
        out_shape=(
            jax.ShapeDtypeStruct((rows, w_qkv.shape[1]), f32),
            jax.ShapeDtypeStruct((rows, part), f32),
            jax.ShapeDtypeStruct((2,) + maps.shape, bf16),
            jax.ShapeDtypeStruct((rows, 2 * rank), bf16),
        ),
        in_specs=[in_hbm, in_hbm] + [in_vmem] * 5,
        out_specs=(in_vmem,) * 4,
        scratch_shapes=[
            pltpu.VMEM(hidden.shape, bf16),
            pltpu.VMEM(w_qkv.shape, bf16),
            pltpu.VMEM(context.shape, bf16),
            pltpu.VMEM((depth, part, part), bf16),
            pltpu.VMEM((depth, rows, part), bf16),
            pltpu.VMEM((depth - 1, rows, part), bf16),
            pltpu.VMEM((depth - 1, rows, part), bf16),
            pltpu.VMEM((2 * rank, hidden.shape[1]), bf16),
            pltpu.VMEM((rows, 2 * rank), f32),
            pltpu.VMEM((tensor_size - 1, rows // tensor_size, 2 * rank), f32),
            dma((2,)),
            dma((2,)),
            dma((2,)),
            dma((depth,)),
            dma((depth,)),
            dma((depth, 2)),
            dma((depth - 1, 2)),
            dma((depth - 1, 2)),
            dma((tensor_size - 1,)),
            dma((tensor_size - 1,)),
            dma((tensor_size,)),
            dma((tensor_size,)),
            dma((depth,)),
            dma((depth,)),
            dma(()),
            dma(()),
        ]
        + [dma((tensor_size - 1,))] * 4,
        compiler_params=pltpu.CompilerParams(
            collective_id=0, has_side_effects=True, vmem_limit_bytes=62 * 1024 * 1024
        ),
        cost_estimate=pl.CostEstimate(
            flops=2 * rows * (hidden.shape[1] * w_qkv.shape[1] + 2 * part * part * depth),
            bytes_accessed=2 * (hidden.size + w_qkv.size + w_out.size + context.size),
            transcendentals=0,
        ),
    )(hidden, w_qkv, context, w_out, maps, a_own, store_row)


def chunk_order(depth):
    rows = []
    for z in range(depth):
        row = []
        for s in range(depth - 1):
            for d, ok in ((z + depth - 1 - s, s >= z), (z - depth + 1 + s, s >= depth - 1 - z)):
                if ok:
                    row.append(d)
        rows.append(row + [z])
    return rows


def token_rows(seg_len, seg_use, row_of_use, tok_rows):
    count = seg_len.shape[0]
    order = jnp.arange(count, dtype=jnp.int32)
    ends = jnp.sum(jnp.where(order[None, :] <= order[:, None], seg_len[None, :], 0), axis=1)
    used = jnp.arange(row_of_use.shape[0], dtype=jnp.int32)
    seg_row = jnp.sum(jnp.where(seg_use[:, None] == used[None, :], row_of_use[None, :], 0), axis=1)
    positions = jnp.arange(tok_rows, dtype=jnp.int32)
    inside = (positions[:, None] >= (ends - seg_len)[None, :]) & (positions[:, None] < ends[None, :])
    return jnp.sum(jnp.where(inside, seg_row[None, :], 0), axis=1)


def plain_shards(
    hidden,
    context,
    w_qkv,
    w_out,
    a_qkv,
    b_qkv,
    a_out,
    b_out,
    seg_len,
    seg_use,
    used_list,
    adapter_slot,
):
    f32, bf16 = jnp.float32, jnp.bfloat16
    tensor_size = lax.axis_size("tensor")
    dp_size = lax.axis_size("dp")
    t = lax.axis_index("tensor")
    dp_rank = lax.axis_index("dp")
    tok_rows, model_width = hidden.shape
    owned, _, rank = a_qkv.shape
    out_part = model_width // tensor_size
    qkv_part = b_qkv.shape[2] // tensor_size
    depth = tensor_size // 2
    z, y = t // 2, t % 2

    used = used_list[dp_rank][:, None] == jnp.arange(adapter_slot.shape[0], dtype=jnp.int32)[None, :]
    row_of_use = jnp.sum(jnp.where(used, adapter_slot[None, :], 0), axis=1)
    store_row = token_rows(seg_len[0], seg_use[0], row_of_use, tok_rows)

    def out_cols(d, side):
        return lax.dynamic_slice_in_dim(w_out, (2 * d + side) * out_part, out_part, 1)

    def partial(d, side):
        return jnp.dot(context, out_cols(d, side), preferred_element_type=f32)

    order = jnp.asarray(chunk_order(depth), jnp.int32)[z]
    swap = [(i, i ^ 1) for i in range(tensor_size)]
    both = [(0, 1), (1, 0)]

    def split(maps, part):
        return jnp.transpose(maps.reshape(owned, rank, tensor_size, part), (2, 0, 1, 3))

    a_out_t = jnp.transpose(a_out, (0, 2, 1))
    sent = jnp.concatenate(
        (split(a_out_t, out_part), split(b_out, out_part), split(b_qkv, qkv_part)), axis=3
    )

    reduced, up, down = [], None, None

    def chosen(d):
        value = reduced[0]
        for k in range(1, len(reduced)):
            value = jnp.where(order[k] == d, reduced[k], value)
        return value

    for k in range(depth):
        mine = lax.ppermute(partial(order[k], 1 - y).astype(bf16), "tensor", swap)
        reduced.append(mine.astype(f32) + partial(order[k], y))
        if k < depth - 1:
            s = k
            outgoing_up = chosen(z + depth - 1 - s)
            outgoing_down = chosen(z - depth + 1 + s)
            if s > 0:
                outgoing_up = outgoing_up + up.astype(f32)
                outgoing_down = outgoing_down + down.astype(f32)
            up_pairs = [(2 * i + j, 2 * i + 2 + j) for i in range(s + 1) for j in range(2)]
            down_pairs = [
                (2 * i + j, 2 * i - 2 + j) for i in range(depth - 1 - s, depth) for j in range(2)
            ]
            up = lax.ppermute(outgoing_up.astype(bf16), "tensor", up_pairs)
            down = lax.ppermute(outgoing_down.astype(bf16), "tensor", down_pairs)
        if k == 0:
            got = lax.all_to_all(sent, "tensor", split_axis=0, concat_axis=0, tiled=True)
            got = got.reshape((tensor_size * owned,) + got.shape[2:])
            other = lax.ppermute(got, "dp", both)
            a_other = lax.ppermute(a_qkv, "dp", both)
    base_out = reduced[-1] + up.astype(f32) + down.astype(f32)

    half = tensor_size * owned
    first = dp_rank * half
    second = (1 - dp_rank) * half
    rows = jnp.arange(half, dtype=jnp.int32)
    row_ids = jnp.concatenate((first + rows, second + rows))
    maps = jnp.concatenate((got, other), axis=0)
    down_out = maps[:, :, :out_part]
    up_out = maps[:, :, out_part : 2 * out_part].reshape(-1, out_part)
    up_qkv = maps[:, :, 2 * out_part :].reshape(-1, qkv_part)
    row_mask = store_row[:, None] == row_ids[None, :]

    own = jnp.arange(owned, dtype=jnp.int32) + t * owned
    own_ids = jnp.concatenate((first + own, second + own))
    own_mask = store_row[:, None] == own_ids[None, :]

    def pick(products, mask):
        shaped = products.reshape(tok_rows, mask.shape[1], rank)
        return jnp.sum(jnp.where(mask[:, :, None], shaped, 0.0), axis=1)

    a_two = jnp.concatenate((a_qkv, a_other), axis=0)
    low_a = jnp.einsum("td,rdk->trk", hidden, a_two, preferred_element_type=f32)
    low_b = jnp.einsum("td,rkd->trk", context, down_out, preferred_element_type=f32)
    low_qkv, low_out = lax.psum((pick(low_a, own_mask), pick(low_b, row_mask)), "tensor")

    def expand(low, up_maps):
        spread = jnp.where(row_mask[:, :, None], low.astype(bf16)[:, None, :], jnp.zeros((), bf16))
        return jnp.dot(spread.reshape(tok_rows, -1), up_maps, preferred_element_type=f32)

    base_qkv = jnp.dot(hidden, w_qkv, preferred_element_type=f32)
    qkv = (base_qkv + expand(low_qkv, up_qkv)).astype(bf16)
    attn_out = (base_out + expand(low_out, up_out)).astype(bf16)
    return (qkv, attn_out)


def shards(
    hidden,
    context,
    w_qkv,
    w_out,
    a_qkv,
    b_qkv,
    a_out,
    b_out,
    seg_len,
    seg_use,
    used_list,
    adapter_slot,
):
    f32, bf16 = jnp.float32, jnp.bfloat16
    tensor_size = lax.axis_size("tensor")
    dp_size = lax.axis_size("dp")
    t = lax.axis_index("tensor")
    dp_rank = lax.axis_index("dp")
    tok_rows, model_width = hidden.shape
    owned, _, rank = a_qkv.shape
    out_part = model_width // tensor_size
    qkv_part = b_qkv.shape[2] // tensor_size
    if tensor_size % 2 or tensor_size < 6 or out_part % 128 or qkv_part % 128 or owned != 1 or rank != 64 or tok_rows % 512:
        return plain_shards(
            hidden, context, w_qkv, w_out, a_qkv, b_qkv, a_out, b_out,
            seg_len, seg_use, used_list, adapter_slot,
        )

    used = used_list[dp_rank][:, None] == jnp.arange(adapter_slot.shape[0], dtype=jnp.int32)[None, :]
    row_of_use = jnp.sum(jnp.where(used, adapter_slot[None, :], 0), axis=1)
    store_row = token_rows(seg_len[0], seg_use[0], row_of_use, tok_rows)

    def split(maps, part):
        return jnp.transpose(maps.reshape(rank, tensor_size, part), (1, 0, 2))

    sent = jnp.concatenate(
        (
            split(jnp.transpose(a_out, (0, 2, 1)), out_part),
            split(b_out, out_part),
            split(b_qkv, qkv_part),
        ),
        axis=2,
    )
    sent = sent.reshape(-1, sent.shape[2])
    store_lanes = jnp.broadcast_to(store_row[:, None], (tok_rows, 2 * rank))
    base_qkv, base_out, got, low = projections(
        tensor_size, hidden, w_qkv, context, w_out, sent, jnp.transpose(a_qkv[0]), store_lanes
    )
    got = got.reshape(-1, got.shape[2])
    up_out = got[:, out_part : 2 * out_part]
    up_qkv = got[:, 2 * out_part :]

    half = tensor_size * owned
    first, second = dp_rank * half, (1 - dp_rank) * half

    def lane_mask(rows):
        return store_row[:, None] == jnp.repeat(rows, rank)[None, :]

    rows = jnp.arange(half, dtype=jnp.int32)
    row_mask = lane_mask(jnp.concatenate((first + rows, second + rows)))

    def expand(start, maps):
        lanes = jnp.arange(row_mask.shape[1], dtype=jnp.int32) % rank + start
        copies = (jnp.arange(2 * rank, dtype=jnp.int32)[:, None] == lanes[None, :]).astype(bf16)
        spread = jnp.dot(low, copies, preferred_element_type=f32).astype(bf16)
        spread = jnp.where(row_mask, spread, jnp.zeros((), bf16))
        return jnp.dot(spread, maps, preferred_element_type=f32)

    qkv = (base_qkv + expand(0, up_qkv)).astype(bf16)
    attn_out = (base_out + expand(rank, up_out)).astype(bf16)
    return (qkv, attn_out)


def solution(mesh):
    placed = (
        P(("groups", "dp"), None),
        P(("groups", "dp"), "tensor"),
        P(None, "tensor"),
        P("tensor", None),
        P(("dp", "tensor"), None, None),
        P(("dp", "tensor"), None, None),
        P(("dp", "tensor"), None, None),
        P(("dp", "tensor"), None, None),
        P(("groups", "dp"), None),
        P(("groups", "dp"), None),
        P("groups", None),
        P(),
    )
    return jax.shard_map(
        shards,
        mesh=mesh,
        in_specs=placed,
        out_specs=(P(("groups", "dp"), "tensor"), P(("groups", "dp"), "tensor")),
        check_vma=False,
    )
```
